512 devices in a mesh: patch: 64 (over x_lo, z, core), head: 8 (over y, x_hi).
Axes of the slice: x: 4 (x_hi: 2, x_lo: 2; x = x_hi * 2 + x_lo), y: 4, z: 16, core: 2. Of those that a mesh axis runs over, the one named last changes fastest.
Arguments:
- query_raw: bfloat16 [12288, 2048], P('patch', 'head'), may hold values from -6 to 6
- key_raw: bfloat16 [12288, 2048], P('patch', 'head'), may hold values from -6 to 6
- value_raw: bfloat16 [12288, 2048], P('patch', 'head'), may hold values from -6 to 6
- stale_pairs: bfloat16 [2, 12288, 2048], P(None, 'patch', 'head'), as said below
- query_gain: float32 [128], replicated, may hold values from 1.2 to 5.5
- key_gain: float32 [128], replicated, may hold values from 1.2 to 5.5
- patch_offsets: int32 [64], P('patch'), may hold values from 0 to 12096, as said below
- attn_gate: float32 [3072], P('head'), may hold values from 1 to 3
- out_weight: bfloat16 [2048, 3072], P(None, 'head'), may hold values from -0.125 to 0.125
Outputs:
- attn_branch: bfloat16 [12288, 3072], P('patch', 'head')
- fresh_keys: bfloat16 [12288, 2048], P('patch', 'head')
The draws below stay inside these ranges and needn't reach their ends.
Inputs may be any that keep to these rules, and one draw needn't show every extreme that they name: `patch_offsets`: every multiple of 192 from 0 to 12096 appears exactly once. `stale_pairs`: index 0 holds keys normed with key_gain and rotated at each token's own position, as fresh_keys are; index 1 holds values like value_raw.
All inputs are finite; a program needn't handle non-finite values.
Results may differ from the reference program's by a relative error of at most 0.017.
Values may be sent and summed in bfloat16 or wider, within the bound.
No kernel may reach another device: no remote copies, remote signals or barrier semaphores. Data moves between devices by JAX's collectives and lax.ppermute only.
A program may use at most 128 MiB of HBM per device.

```python
import jax
import jax.numpy as jnp
from jax import lax

D = 3072
HEADS = 16
HEAD_DIM = 128
TOK_DEV = 192
PATCHES = 64
TOKENS = 12288


def shared_key_gain(key, lower, upper):
    gain_key = jax.random.fold_in(key, 12)
    return jax.random.uniform(gain_key, (HEAD_DIM,), jnp.float32, lower, upper)


def shared_offsets(key):
    offset_key = jax.random.fold_in(key, 13)
    return (jax.random.permutation(offset_key, PATCHES) * TOK_DEV).astype(jnp.int32)


def rotate_rows(raw_heads, gain_vector, positions):
    head_width = raw_heads.shape[-1]
    halfway = head_width // 2
    squares = jnp.mean(raw_heads * raw_heads, axis=-1, keepdims=True)
    normed = raw_heads * lax.rsqrt(squares + 1e-06) * gain_vector
    frequency = jnp.exp(-(2.0 * jnp.arange(halfway, dtype=jnp.float32) / head_width) * jnp.log(256.0))
    angles = positions.astype(jnp.float32)[..., None] * frequency
    cosine = jnp.cos(angles)[..., None, :]
    sinusoid = jnp.sin(angles)[..., None, :]
    leading = normed[..., :halfway]
    trailing = normed[..., halfway:]
    return jnp.concatenate([leading * cosine - trailing * sinusoid, trailing * cosine + leading * sinusoid], axis=-1)


def draw_query_gain(key, part):
    key = jax.random.fold_in(key, 11)
    return jax.random.uniform(key, (HEAD_DIM,), jnp.float32, 1.2, 1.8)


def draw_key_gain(key, part):
    return shared_key_gain(key, 1.2, 1.8)


def draw_patch_offsets(key, part):
    return shared_offsets(key)


def draw_stale_pairs(key, part):
    gain_vector = shared_key_gain(key, 1.2, 1.8)
    offsets = shared_offsets(key)
    key = jax.random.fold_in(key, 14)
    key_part, value_part = jax.random.split(key)
    positions = offsets[:, None] + jnp.arange(TOK_DEV, dtype=jnp.int32)[None, :]
    raw_keys = jnp.clip(jax.random.normal(key_part, (PATCHES, TOK_DEV, HEADS, HEAD_DIM), jnp.float32), -6.0, 6.0)
    stale_keys = rotate_rows(raw_keys, gain_vector, positions).reshape(TOKENS, HEADS * HEAD_DIM)
    stale_values = jnp.clip(jax.random.normal(value_part, (TOKENS, HEADS * HEAD_DIM), jnp.float32), -6.0, 6.0)
    return jnp.stack([stale_keys, stale_values]).astype(jnp.bfloat16)


def levels(key, shape, pieces, least, high):
    level, own = 1.0, jax.random.fold_in(key, 6)
    for axis_at, parts in pieces:
        draws = jnp.exp(jax.random.uniform(jax.random.fold_in(own, axis_at), (parts,), jnp.float32, least / len(pieces), high / len(pieces)))
        level = level * jnp.repeat(draws, shape[axis_at] // parts).reshape([-1 if axis == axis_at else 1 for axis in range(len(shape))])
    return level


def centred(stream_key, shape, deviation, limit, cuts=(), kind=jnp.bfloat16):
    loudness = levels(stream_key, shape, cuts, -0.22, 0.18) if cuts else 1.0
    entries = jax.random.normal(stream_key, shape, jnp.float32) * deviation * loudness
    return jnp.minimum(jnp.maximum(entries, -limit), limit).astype(kind)


def setup_inputs(seed: int = 0) -> dict:
    splits = jax.random.split(jax.random.key(seed), 10)
    query_raw = centred(splits[0], (TOKENS, HEADS * HEAD_DIM), 1.0, 6.0, ((0, 64), (1, 8)))
    key_raw = centred(splits[1], (TOKENS, HEADS * HEAD_DIM), 1.0, 6.0, ((0, 64), (1, 8)))
    value_raw = centred(splits[2], (TOKENS, HEADS * HEAD_DIM), 1.0, 6.0, ((0, 64), (1, 8)))
    stale_pairs = draw_stale_pairs(jax.random.fold_in(splits[9], 71), 0)
    query_gain = draw_query_gain(jax.random.fold_in(splits[9], 71), 0)
    key_gain = draw_key_gain(jax.random.fold_in(splits[9], 71), 0)
    patch_offsets = draw_patch_offsets(jax.random.fold_in(splits[9], 71), 0)
    attn_gate = jnp.clip(1.0 + 2.0 * jax.random.uniform(splits[7], (D,), jnp.float32) ** levels(splits[7], (D,), ((0, 8),), -0.2, 0.2), 1.0, 3.0)
    out_weight = centred(splits[8], (HEADS * HEAD_DIM, D), (HEADS * HEAD_DIM) ** -0.5, 0.125, ((1, 8),))
    return {"query_raw": query_raw, "key_raw": key_raw, "value_raw": value_raw, "stale_pairs": stale_pairs, "query_gain": query_gain, "key_gain": key_gain, "patch_offsets": patch_offsets, "attn_gate": attn_gate, "out_weight": out_weight}


def rotated_norm(raw_heads, gain_vector, positions):
    head_width = raw_heads.shape[-1]
    halfway = head_width // 2
    squares = lax.optimization_barrier(jnp.mean(raw_heads * raw_heads, axis=-1, keepdims=True))
    normed = raw_heads * lax.rsqrt(squares + 1e-06) * gain_vector
    frequency = jnp.exp(-(2.0 * jnp.arange(halfway, dtype=jnp.float32) / head_width) * jnp.log(256.0))
    angles = positions.astype(jnp.float32)[..., None] * frequency
    cosine = jnp.cos(angles)[..., None, :]
    sinusoid = jnp.sin(angles)[..., None, :]
    leading = normed[..., :halfway]
    trailing = normed[..., halfway:]
    return jnp.concatenate([leading * cosine - trailing * sinusoid, trailing * cosine + leading * sinusoid], axis=-1)

def reference(query_raw, key_raw, value_raw, stale_pairs, query_gain, key_gain, patch_offsets, attn_gate, out_weight):
    head_shape = (PATCHES, TOK_DEV, HEADS, HEAD_DIM)
    positions = patch_offsets[:, None] + jnp.arange(TOK_DEV, dtype=jnp.int32)[None, :]
    queries = rotated_norm(query_raw.astype(jnp.float32).reshape(head_shape), query_gain, positions).astype(jnp.bfloat16)
    fresh_keys = rotated_norm(key_raw.astype(jnp.float32).reshape(head_shape), key_gain, positions).astype(jnp.bfloat16)
    values_now = value_raw.reshape(head_shape)
    stale_keys = stale_pairs[0].reshape(head_shape)
    stale_values = stale_pairs[1].reshape(head_shape)
    patch_ids = jnp.arange(PATCHES, dtype=jnp.int32)

    def one_patch(patch_index):
        chosen = (patch_ids == patch_index)[:, None, None, None]
        keys_seen = jnp.where(chosen, fresh_keys[patch_index][None], stale_keys).reshape(TOKENS, HEADS, HEAD_DIM)
        values_seen = jnp.where(chosen, values_now[patch_index][None], stale_values).reshape(TOKENS, HEADS, HEAD_DIM)
        scores = jnp.einsum('qhd,khd->hqk', queries[patch_index].astype(jnp.float32), keys_seen.astype(jnp.float32)) * HEAD_DIM ** (-0.5)
        highest = lax.optimization_barrier(jnp.max(scores, axis=-1, keepdims=True))
        weights = jnp.exp(scores - highest)
        totals = lax.optimization_barrier(jnp.sum(weights, axis=-1))
        rounded = lax.optimization_barrier(weights.astype(jnp.bfloat16)).astype(jnp.float32)
        summed = jnp.einsum('hqk,khd->qhd', rounded, values_seen.astype(jnp.float32))
        return (summed / jnp.transpose(totals)[:, :, None]).astype(jnp.bfloat16)
    attended = lax.map(one_patch, patch_ids).reshape(TOKENS, HEADS * HEAD_DIM)
    projected = jnp.dot(attended, out_weight, preferred_element_type=jnp.float32)
    attn_branch = (projected * attn_gate[None, :]).astype(jnp.bfloat16)
    return (attn_branch, fresh_keys.reshape(TOKENS, HEADS * HEAD_DIM))
```

```python
import functools

import jax
import jax.numpy as jnp
import numpy as np
from jax import lax
from jax.experimental import pallas as pl
from jax.experimental.pallas import tpu as pltpu
from jax.sharding import PartitionSpec as P

BF16 = jnp.bfloat16
F32 = jnp.float32
TOKENS = 192
HEAD = 128
WIDTH = 256
HEADS_HERE = 2
STAT_ROWS = 16
ROWS_SENT = TOKENS + STAT_ROWS
CHUNK = 4
LOG2E = 1.4426950408889634
VMEM_LIMIT = 48 * 1024 * 1024

QUERY_GROUPS = [
    [x * 32 + (2 * pair + z) * 2 + core for z in range(2) for x in range(2)]
    for pair in range(8)
    for core in range(2)
]
KEY_GROUPS = [
    [x * 32 + (2 * step + z) * 2 + core for step in range(8) for core in range(2)]
    for x in range(2)
    for z in range(2)
]


def place_in(groups):
    place = np.zeros(64, np.int32)
    for group in groups:
        for at, member in enumerate(group):
            place[member] = at
    return jnp.asarray(place)


def prepare_body(q_ref, k_ref, q_gain_ref, k_gain_ref, cos_ref, sin_ref, q_out, k_out):
    cosine, signed_sine = cos_ref[...], sin_ref[...]
    for raw, gain, out in ((q_ref, q_gain_ref, q_out), (k_ref, k_gain_ref, k_out)):
        for h in range(HEADS_HERE):
            cols = slice(h * HEAD, (h + 1) * HEAD)
            x = raw[:, cols].astype(F32)
            squares = jnp.mean(x * x, axis=-1, keepdims=True)
            n = x * lax.rsqrt(squares + 1e-06) * gain[...]
            out[:, cols] = (n * cosine + pltpu.roll(n, HEAD // 2, 1) * signed_sine).astype(BF16)


def prepare(query_raw, key_raw, query_gain, key_gain, cosine, signed_sine):
    shape = jax.ShapeDtypeStruct((TOKENS, WIDTH), BF16)
    return pl.pallas_call(
        prepare_body,
        out_shape=(shape, shape),
        name="norm_rotate",
    )(query_raw, key_raw, query_gain[None], key_gain[None], cosine, signed_sine)


def scores_of(q, k):
    return lax.dot_general(q, k, (((1,), (1,)), ((), ())), preferred_element_type=F32)


def attend_body(
    place_ref, q_ref, kv_ref, fresh_k_ref, fresh_v_ref, out_ref, peak_ref, total_ref, sum_ref
):
    step = pl.program_id(0)
    steps = pl.num_programs(0)
    scale = HEAD**-0.5 * LOG2E
    rows = q_ref.shape[0]
    keys = CHUNK * TOKENS
    block = 256

    def first(q, k, v):
        s = scores_of(q, k)
        peak = jnp.max(s, axis=-1, keepdims=True) * scale
        p = jnp.exp2(s * scale - peak)
        total = jnp.sum(p, axis=-1, keepdims=True)
        return peak, total, jnp.dot(p.astype(BF16), v, preferred_element_type=F32)

    def store(h, at, size, peak, total, acc):
        peak_ref[h, pl.ds(at, size), :] = jnp.broadcast_to(peak, (size, HEAD))
        total_ref[h, pl.ds(at, size), :] = jnp.broadcast_to(total, (size, HEAD))
        sum_ref[h, pl.ds(at, size), :] = acc

    @pl.when(step == 0)
    def _():
        mine = pl.multiple_of(place_ref[0] * TOKENS, TOKENS)
        slot = lax.rem(place_ref[1], CHUNK)
        for h in range(HEADS_HERE):
            cols = slice(h * HEAD, (h + 1) * HEAD)
            k = kv_ref[:, 0, :, cols].reshape(keys, HEAD)
            v = kv_ref[:, 1, :, cols].reshape(keys, HEAD)
            for r in range(rows // block):
                store(h, r * block, block, *first(q_ref[r * block : (r + 1) * block, cols], k, v))
            fresh_k, fresh_v = fresh_k_ref[:, cols], fresh_v_ref[:, cols]
            k = jnp.concatenate(
                [jnp.where(slot == t, fresh_k, kv_ref[t, 0, :, cols]) for t in range(CHUNK)]
            )
            v = jnp.concatenate(
                [jnp.where(slot == t, fresh_v, kv_ref[t, 1, :, cols]) for t in range(CHUNK)]
            )
            store(h, mine, TOKENS, *first(q_ref[pl.ds(mine, TOKENS), cols], k, v))

    @pl.when(step > 0)
    def _():
        for h in range(HEADS_HERE):
            cols = slice(h * HEAD, (h + 1) * HEAD)
            k = kv_ref[:, 0, :, cols].reshape(keys, HEAD)
            v = kv_ref[:, 1, :, cols].reshape(keys, HEAD)
            for r in range(rows // block):
                at = slice(r * block, (r + 1) * block)
                s = scores_of(q_ref[at, cols], k)
                before = peak_ref[h, at, :1]
                peak = jnp.maximum(before, jnp.max(s, axis=-1, keepdims=True) * scale)
                p = jnp.exp2(s * scale - peak)
                shrink = jnp.exp2(before - peak)
                total = total_ref[h, at, :1] * shrink + jnp.sum(p, axis=-1, keepdims=True)
                acc = sum_ref[h, at, :] * shrink + jnp.dot(
                    p.astype(BF16), v, preferred_element_type=F32
                )
                store(h, r * block, block, peak, total, acc)

    @pl.when(step == steps - 1)
    def _():
        lane = lax.broadcasted_iota(jnp.int32, (TOKENS, HEAD), 1)
        for g in range(rows // TOKENS):
            at = slice(g * TOKENS, (g + 1) * TOKENS)
            stats = jnp.zeros((TOKENS, HEAD), F32)
            for h in range(HEADS_HERE):
                cols = slice(h * HEAD, (h + 1) * HEAD)
                total = total_ref[h, at, :]
                out_ref[g, :TOKENS, cols] = (sum_ref[h, at, :] / total).astype(BF16)
                level = peak_ref[h, at, :] + jnp.log2(total)
                high = level.astype(BF16).astype(F32)
                middle = (level - high).astype(BF16).astype(F32)
                low = level - high - middle
                for piece, value in enumerate((high, middle, low)):
                    stats = jnp.where(lane == 3 * h + piece, value, stats)
            flat = jnp.transpose(stats)[:STAT_ROWS]
            out_ref[g, TOKENS:, :] = jnp.concatenate(
                [flat, jnp.zeros((STAT_ROWS, WIDTH - TOKENS), F32)], axis=1
            ).astype(BF16)


def attend(places, queries, pairs, fresh_keys, values_now):
    rows = queries.shape[0]
    steps = pairs.shape[0] // CHUNK
    whole = lambda i, place: (0, 0)
    return pl.pallas_call(
        attend_body,
        grid_spec=pltpu.PrefetchScalarGridSpec(
            num_scalar_prefetch=1,
            grid=(steps,),
            in_specs=[
                pl.BlockSpec((rows, WIDTH), whole),
                pl.BlockSpec(
                    (CHUNK, 2, TOKENS, WIDTH),
                    lambda i, place: (lax.rem(place[1] // CHUNK + i, steps), 0, 0, 0),
                ),
                pl.BlockSpec((TOKENS, WIDTH), whole),
                pl.BlockSpec((TOKENS, WIDTH), whole),
            ],
            out_specs=pl.BlockSpec(
                (rows // TOKENS, ROWS_SENT, WIDTH), lambda i, place: (0, 0, 0)
            ),
            scratch_shapes=[pltpu.VMEM((HEADS_HERE, rows, HEAD), F32)] * 3,
        ),
        out_shape=jax.ShapeDtypeStruct((rows // TOKENS, ROWS_SENT, WIDTH), BF16),
        compiler_params=pltpu.CompilerParams(vmem_limit_bytes=VMEM_LIMIT),
        name="attend",
    )(places, queries, pairs, fresh_keys, values_now)


def merge_body(parts_ref, out_ref):
    count = parts_ref.shape[0]
    levels = []
    for g in range(count):
        flat = parts_ref[g, TOKENS:, :].astype(F32)
        tall = jnp.concatenate([flat, jnp.zeros((HEAD - STAT_ROWS, WIDTH), F32)])
        levels.append(jnp.transpose(tall)[:TOKENS])
    for h in range(HEADS_HERE):
        cols = slice(h * HEAD, (h + 1) * HEAD)
        level = [
            s[:, 3 * h : 3 * h + 1] + s[:, 3 * h + 1 : 3 * h + 2] + s[:, 3 * h + 2 : 3 * h + 3]
            for s in levels
        ]
        top = functools.reduce(jnp.maximum, level)
        weights = [jnp.exp2(one - top) for one in level]
        acc = sum(
            w * parts_ref[g, :TOKENS, cols].astype(F32) for g, w in enumerate(weights)
        )
        merged = (acc / sum(weights)).astype(BF16)
        for copy in range(out_ref.shape[0]):
            out_ref[copy, :, cols] = merged


def merge(parts, copies):
    return pl.pallas_call(
        merge_body,
        out_shape=jax.ShapeDtypeStruct((copies, TOKENS, WIDTH), BF16),
        name="merge",
    )(parts)


def project_body(parts_ref, weight_ref, gate_ref, out_ref):
    acc = jnp.dot(parts_ref[0], weight_ref[:WIDTH], preferred_element_type=F32)
    for g in range(1, parts_ref.shape[0]):
        acc += jnp.dot(
            parts_ref[g], weight_ref[g * WIDTH : (g + 1) * WIDTH], preferred_element_type=F32
        )
    out_ref[...] = (acc * gate_ref[...]).astype(BF16)


def project(parts, out_weight, attn_gate):
    return pl.pallas_call(
        project_body,
        out_shape=jax.ShapeDtypeStruct((TOKENS, out_weight.shape[1]), BF16),
        compiler_params=pltpu.CompilerParams(vmem_limit_bytes=VMEM_LIMIT),
        name="project",
    )(parts, out_weight, attn_gate[None])


def shards(
    query_raw,
    key_raw,
    value_raw,
    stale_pairs,
    query_gain,
    key_gain,
    patch_offsets,
    attn_gate,
    out_weight,
):
    pairs = lax.all_gather(stale_pairs, "patch", axis=0, axis_index_groups=KEY_GROUPS)
    positions = patch_offsets[0] + jnp.arange(TOKENS, dtype=jnp.int32)
    frequency = jnp.exp(
        -(2.0 * jnp.arange(HEAD // 2, dtype=F32) / HEAD) * jnp.log(256.0)
    )
    angles = positions.astype(F32)[:, None] * frequency
    cosine, sine = jnp.cos(angles), jnp.sin(angles)
    queries, fresh_keys = prepare(
        query_raw,
        key_raw,
        query_gain,
        key_gain,
        jnp.concatenate([cosine, cosine], axis=1),
        jnp.concatenate([-sine, sine], axis=1),
    )
    group_queries = lax.all_gather(
        queries, "patch", axis=0, tiled=True, axis_index_groups=QUERY_GROUPS
    )
    me = lax.axis_index("patch")
    places = jnp.stack([place_in(QUERY_GROUPS)[me], place_in(KEY_GROUPS)[me]])
    parts = attend(places, group_queries, pairs, fresh_keys, value_raw)
    parts = lax.all_to_all(
        parts, "patch", split_axis=0, concat_axis=0, tiled=True, axis_index_groups=QUERY_GROUPS
    )
    copies = merge(parts, 8)
    all_heads = lax.all_to_all(copies, "head", split_axis=0, concat_axis=0, tiled=True)
    return (project(all_heads, out_weight, attn_gate), fresh_keys)


def solution(mesh):
    return jax.shard_map(
        shards,
        mesh=mesh,
        in_specs=(
            P("patch", "head"),
            P("patch", "head"),
            P("patch", "head"),
            P(None, "patch", "head"),
            P(),
            P(),
            P("patch"),
            P("head"),
            P(None, "head"),
        ),
        out_specs=(P("patch", "head"), P("patch", "head")),
        check_vma=False,
    )
```

```python
import functools

import jax
import jax.numpy as jnp
from jax import lax
from jax.experimental import pallas as pl
from jax.experimental.pallas import tpu as pltpu
from jax.sharding import PartitionSpec as P

BF16 = jnp.bfloat16
F32 = jnp.float32
TOKENS = 192
HEAD = 128
WIDTH = 256
HEADS_HERE = 2
STAT_ROWS = 16
ROWS_SENT = TOKENS + STAT_ROWS
LOG2E = 1.4426950408889634
VMEM_LIMIT = 48 * 1024 * 1024

PATCHES = 64
CORES = [[i, i + 1] for i in range(0, PATCHES, 2)]
QUERY_GROUPS = [
    [x * 32 + (2 * pair + z) * 2 + core for core in range(2) for x in range(2) for z in range(2)]
    for pair in range(8)
]


def swapped(bit):
    return [(i, i ^ bit) for i in range(PATCHES)]


def ring_swaps(first):
    pairs = []
    for i in range(PATCHES):
        z, core = i % 32 // 2, i % 2
        odd = z // 2 % 2
        by = 2 - 4 * odd if first == (core == 0) else 4 * odd - 2
        pairs.append((i, i // 32 * 32 + (z + by) % 16 * 2 + core))
    return pairs


def prepare_body(
    core_ref, q_ref, k_ref, v_ref, q_gain_ref, k_gain_ref, cos_ref, sin_ref, k_out, mine_out, send_out
):
    cosine, signed_sine = cos_ref[...], sin_ref[...]
    first = core_ref[0] == 0

    def put(part, heads):
        mine_out[part] = jnp.where(first, heads[0], heads[1])
        send_out[part] = jnp.where(first, heads[1], heads[0])

    for part, (raw, gain) in enumerate(((q_ref, q_gain_ref), (k_ref, k_gain_ref))):
        heads = []
        for h in range(HEADS_HERE):
            cols = slice(h * HEAD, (h + 1) * HEAD)
            x = raw[:, cols].astype(F32)
            squares = jnp.mean(x * x, axis=-1, keepdims=True)
            n = x * lax.rsqrt(squares + 1e-06) * gain[...]
            turned = (n * cosine + pltpu.roll(n, HEAD // 2, 1) * signed_sine).astype(BF16)
            heads.append(turned)
            if part == 1:
                k_out[:, cols] = turned
        put(part, heads)
    put(2, [v_ref[:, :HEAD], v_ref[:, HEAD:]])


def prepare(core, query_raw, key_raw, value_raw, query_gain, key_gain, cosine, signed_sine):
    halves = jax.ShapeDtypeStruct((3, TOKENS, HEAD), BF16)
    return pl.pallas_call(
        prepare_body,
        in_specs=[pl.BlockSpec(memory_space=pltpu.SMEM)]
        + [pl.BlockSpec(memory_space=pltpu.VMEM)] * 7,
        out_shape=(jax.ShapeDtypeStruct((TOKENS, WIDTH), BF16), halves, halves),
        name="norm_rotate",
    )(core, query_raw, key_raw, value_raw, query_gain[None], key_gain[None], cosine, signed_sine)


def attend_body(share_count, begins, ends, *refs):
    refs = list(refs)
    take = lambda count: [refs.pop(0) for _ in range(count)]
    scale = HEAD**-0.5 * LOG2E
    place_ref = take(1)[0] if begins or ends else None
    q_refs = take(2)
    fresh_refs = take(2) if begins else None
    before = None if begins else take(3)
    shares = take(share_count)
    half = q_refs[0].shape[0]

    def rows_of(part, patch=None):
        if ends:
            picked = [shares[part][core] for core in range(2)]
        else:
            picked = [share[part, core] for share in shares for core in range(2)]
        if patch is not None:
            at = jnp.bitwise_xor(place_ref[1], patch)
            new = fresh_refs[patch][1 + part]
            picked = [jnp.where(at == core, new, old) for core, old in enumerate(picked)]
        return jnp.concatenate(picked)

    size = 2 * TOKENS
    blocks = [(at, size, None) for at in range(0, 2 * half, size)]
    if begins:
        blocks[:1] = [(0, TOKENS, 0), (TOKENS, TOKENS, 1)]
    usual = rows_of(0), rows_of(1)

    def scores_of(block):
        at, size, patch = block
        k = usual[0] if patch is None else rows_of(0, patch)
        q = q_refs[at // half][at % half : at % half + size, :]
        return lax.dot_general(q, k, (((1,), (1,)), ((), ())), preferred_element_type=F32)

    def finish(at, size, peak, total, acc):
        total = jnp.sum(total, axis=-1, keepdims=True)
        level = peak + jnp.log2(total)
        high = level.astype(BF16).astype(F32)
        middle = (level - high).astype(BF16).astype(F32)
        low = level - high - middle
        lane = lax.broadcasted_iota(jnp.int32, (size, HEAD), 1)
        packed = jnp.where(lane == 0, high, jnp.where(lane == 1, middle, low))
        out = (acc / total).astype(BF16)
        for g in range(at // TOKENS, (at + size) // TOKENS):
            rows = slice(g * TOKENS - at, (g + 1) * TOKENS - at)
            to = jnp.bitwise_xor(place_ref[1], g % 2) * 4 + jnp.bitwise_xor(place_ref[0], g // 2)
            refs[0][to, :TOKENS, :] = out[rows]
            flat = jnp.transpose(packed[rows])[:8]
            rest = jnp.concatenate([flat[:, HEAD:], jnp.zeros((8, 2 * HEAD - TOKENS), F32)], axis=1)
            refs[0][to, TOKENS:, :] = jnp.concatenate([flat[:, :HEAD], rest]).astype(BF16)

    following = scores_of(blocks[0])
    for index, (at, size, patch) in enumerate(blocks):
        s = following
        if index + 1 < len(blocks):
            following = scores_of(blocks[index + 1])
        rows = slice(at, at + size)
        tiles = [s[:, t * HEAD : (t + 1) * HEAD] for t in range(s.shape[1] // HEAD)]
        peak = jnp.max(functools.reduce(jnp.maximum, tiles), axis=-1, keepdims=True) * scale
        if begins:
            peak = jnp.broadcast_to(peak, (size, HEAD))
        else:
            peak_before = before[0][rows, :]
            peak = jnp.maximum(peak_before, peak)
        tiles = [jnp.exp2(tile * scale - peak) for tile in tiles]
        total = functools.reduce(jnp.add, tiles)
        p = jnp.concatenate([tile.astype(BF16) for tile in tiles], axis=1)
        v = usual[1] if patch is None else rows_of(1, patch)
        acc = jnp.dot(p, v, preferred_element_type=F32)
        if not begins:
            shrink = jnp.exp2(peak_before - peak)
            total += before[1][rows, :] * shrink
            acc += before[2][rows, :] * shrink
        if ends:
            finish(at, size, peak, total, acc)
        else:
            for ref, value in zip(refs, (peak, total, acc), strict=True):
                ref[rows, :] = value


def attend(queries, shares, fresh=(), state=(), place=None, ends=False):
    rows = 2 * queries[0].shape[0]
    begins = bool(fresh)
    operands = [*queries, *fresh, *state, *shares]
    specs = [pl.BlockSpec(memory_space=pltpu.VMEM)] * len(operands)
    if begins or ends:
        operands.insert(0, place)
        specs.insert(0, pl.BlockSpec(memory_space=pltpu.SMEM))
    if ends:
        out_shape = jax.ShapeDtypeStruct((rows // TOKENS, ROWS_SENT, HEAD), BF16)
    else:
        out_shape = (jax.ShapeDtypeStruct((rows, HEAD), F32),) * 3
    key_count = 2 * TOKENS * (1 if ends else len(shares))
    return pl.pallas_call(
        functools.partial(attend_body, len(shares), begins, ends),
        in_specs=specs,
        out_shape=out_shape,
        compiler_params=pltpu.CompilerParams(vmem_limit_bytes=VMEM_LIMIT),
        cost_estimate=pl.CostEstimate(
            flops=4 * rows * key_count * HEAD,
            bytes_accessed=12 * rows * HEAD,
            transcendentals=rows * key_count,
        ),
        name="attend",
    )(*operands)


def merge_body(parts_ref, out_ref):
    count = parts_ref.shape[0]
    chips = count // HEADS_HERE
    weights = []
    for h in range(HEADS_HERE):
        levels = []
        for g in range(h * chips, (h + 1) * chips):
            flat = parts_ref[g, TOKENS:, :].astype(F32)
            wide = jnp.concatenate([flat[:8], flat[8:]], axis=1)
            levels.append(wide[0:1] + wide[1:2] + wide[2:3])
        top = functools.reduce(jnp.maximum, levels)
        weights += [jnp.exp2(one - top) for one in levels]
        whole = sum(weights[h * chips :])
        weights[h * chips :] = [one / whole for one in weights[h * chips :]]
    wide = jnp.concatenate(weights + [jnp.zeros((HEAD - count, 2 * HEAD), F32)])
    columns = jnp.transpose(wide)[:TOKENS]
    for h in range(HEADS_HERE):
        cols = slice(h * HEAD, (h + 1) * HEAD)
        merged = sum(
            columns[:, g : g + 1] * parts_ref[g, :TOKENS, :].astype(F32)
            for g in range(h * chips, (h + 1) * chips)
        ).astype(BF16)
        for copy in range(out_ref.shape[0]):
            out_ref[copy, :, cols] = merged


def merge(parts, copies):
    return pl.pallas_call(
        merge_body,
        out_shape=jax.ShapeDtypeStruct((copies, TOKENS, WIDTH), BF16),
        name="merge",
    )(parts)


def project_body(parts_ref, weight_ref, gate_ref, out_ref):
    acc = jnp.dot(parts_ref[0], weight_ref[:WIDTH], preferred_element_type=F32)
    for g in range(1, parts_ref.shape[0]):
        acc += jnp.dot(
            parts_ref[g], weight_ref[g * WIDTH : (g + 1) * WIDTH], preferred_element_type=F32
        )
    out_ref[...] = (acc * gate_ref[...]).astype(BF16)


def project(parts, out_weight, attn_gate):
    return pl.pallas_call(
        project_body,
        out_shape=jax.ShapeDtypeStruct((TOKENS, out_weight.shape[1]), BF16),
        compiler_params=pltpu.CompilerParams(vmem_limit_bytes=VMEM_LIMIT),
        name="project",
    )(parts, out_weight, attn_gate[None])


def shards(
    query_raw,
    key_raw,
    value_raw,
    stale_pairs,
    query_gain,
    key_gain,
    patch_offsets,
    attn_gate,
    out_weight,
):
    me = lax.axis_index("patch").astype(jnp.int32)
    core = me % 2

    def own_head(both):
        both = jnp.swapaxes(both, 0, 1)
        return lax.dynamic_slice_in_dim(both, core * HEAD, HEAD, axis=3)

    def over_cores(x):
        return lax.all_gather(x, "patch", axis=0, axis_index_groups=CORES)

    share = own_head(over_cores(stale_pairs))
    one, other = ring_swaps(True), ring_swaps(False)
    over_one, over_other = [share], [share]

    def step():
        block = over_other[-1]
        over_other.append(lax.ppermute(over_one[-1], "patch", other))
        over_one.append(lax.ppermute(block, "patch", one))

    step()
    step()
    step()
    positions = patch_offsets[0] + jnp.arange(TOKENS, dtype=jnp.int32)
    frequency = jnp.exp(
        -(2.0 * jnp.arange(HEAD // 2, dtype=F32) / HEAD) * jnp.log(256.0)
    )
    angles = positions.astype(F32)[:, None] * frequency
    cosine, sine = jnp.cos(angles), jnp.sin(angles)
    fresh_keys, mine, send = prepare(
        core[None],
        query_raw,
        key_raw,
        value_raw,
        query_gain,
        key_gain,
        jnp.concatenate([cosine, cosine], axis=1),
        jnp.concatenate([-sine, sine], axis=1),
    )
    theirs = lax.ppermute(send, "patch", swapped(1))
    near = jnp.concatenate([mine[0], theirs[0]])
    near = jnp.concatenate([near, lax.ppermute(near, "patch", swapped(2))])
    queries = (near, lax.ppermute(near, "patch", swapped(32)))
    place = jnp.stack([(me // 32) * 2 + (me // 2) % 2, core])
    state = attend(queries, [share], fresh=(mine, theirs), place=place)
    state = attend(queries, [over_one[1], over_other[1]], state=state)
    far_keys = lax.ppermute(over_other[3][0], "patch", one)
    far_values = lax.ppermute(over_one[3][1], "patch", other)
    state = attend(queries, [over_one[2], over_other[2]], state=state)
    state = attend(queries, [over_one[3], over_other[3]], state=state)
    parts = attend(queries, [far_keys, far_values], state=state, place=place, ends=True)
    parts = lax.all_to_all(
        parts, "patch", split_axis=0, concat_axis=0, tiled=True, axis_index_groups=QUERY_GROUPS
    )
    copies = merge(parts, 8)
    all_heads = lax.all_to_all(copies, "head", split_axis=0, concat_axis=0, tiled=True)
    return (project(all_heads, out_weight, attn_gate), fresh_keys)


def solution(mesh):
    return jax.shard_map(
        shards,
        mesh=mesh,
        in_specs=(
            P("patch", "head"),
            P("patch", "head"),
            P("patch", "head"),
            P(None, "patch", "head"),
            P(),
            P(),
            P("patch"),
            P("head"),
            P(None, "head"),
        ),
        out_specs=(P("patch", "head"), P("patch", "head")),
        check_vma=False,
    )
```

```python
import functools

import jax
import jax.numpy as jnp
from jax import lax
from jax.experimental import pallas as pl
from jax.experimental.pallas import tpu as pltpu
from jax.sharding import PartitionSpec as P

BF16 = jnp.bfloat16
F32 = jnp.float32
TOKENS = 192
HEAD = 128
WIDTH = 256
HEADS_HERE = 2
STAT_ROWS = 16
ROWS_SENT = TOKENS + STAT_ROWS
LOG2E = 1.4426950408889634
VMEM_LIMIT = 20 * 1024 * 1024

PATCHES = 64
CORES = [[i, i + 1] for i in range(0, PATCHES, 2)]
QUERY_GROUPS = [
    [x * 32 + (2 * pair + z) * 2 + core for core in range(2) for x in range(2) for z in range(2)]
    for pair in range(8)
]


def swapped(bit):
    return [(i, i ^ bit) for i in range(PATCHES)]


def ring_swaps(first):
    pairs = []
    for i in range(PATCHES):
        z, core = i % 32 // 2, i % 2
        odd = z // 2 % 2
        by = 2 - 4 * odd if first == (core == 0) else 4 * odd - 2
        pairs.append((i, i // 32 * 32 + (z + by) % 16 * 2 + core))
    return pairs


def prepare_body(
    core_ref, q_ref, k_ref, v_ref, q_gain_ref, k_gain_ref, cos_ref, sin_ref, k_out, mine_out, send_out
):
    cosine, signed_sine = cos_ref[...], sin_ref[...]
    first = core_ref[0] == 0

    def put(part, heads):
        mine_out[part] = jnp.where(first, heads[0], heads[1])
        send_out[part] = jnp.where(first, heads[1], heads[0])

    for part, (raw, gain) in enumerate(((q_ref, q_gain_ref), (k_ref, k_gain_ref))):
        heads = []
        for h in range(HEADS_HERE):
            cols = slice(h * HEAD, (h + 1) * HEAD)
            x = raw[:, cols].astype(F32)
            squares = jnp.mean(x * x, axis=-1, keepdims=True)
            n = x * lax.rsqrt(squares + 1e-06) * gain[...]
            turned = (n * cosine + pltpu.roll(n, HEAD // 2, 1) * signed_sine).astype(BF16)
            heads.append(turned)
            if part == 1:
                k_out[:, cols] = turned
        put(part, heads)
    put(2, [v_ref[:, :HEAD], v_ref[:, HEAD:]])


def prepare(core, query_raw, key_raw, value_raw, query_gain, key_gain, cosine, signed_sine):
    halves = jax.ShapeDtypeStruct((3, TOKENS, HEAD), BF16)
    return pl.pallas_call(
        prepare_body,
        in_specs=[pl.BlockSpec(memory_space=pltpu.SMEM)]
        + [pl.BlockSpec(memory_space=pltpu.VMEM)] * 7,
        out_shape=(jax.ShapeDtypeStruct((TOKENS, WIDTH), BF16), halves, halves),
        name="norm_rotate",
    )(core, query_raw, key_raw, value_raw, query_gain[None], key_gain[None], cosine, signed_sine)


def attend_body(share_count, begins, ends, *refs):
    refs = list(refs)
    take = lambda count: [refs.pop(0) for _ in range(count)]
    scale = HEAD**-0.5 * LOG2E
    place_ref = take(1)[0] if begins or ends else None
    q_refs = take(2)
    fresh_refs = take(2) if begins else None
    before = None if begins else take(3)
    shares = take(share_count)
    half = q_refs[0].shape[0]

    def rows_of(part, patch=None):
        if ends:
            picked = [shares[part][core] for core in range(2)]
        else:
            picked = [share[part, core] for share in shares for core in range(2)]
        if patch is not None:
            at = jnp.bitwise_xor(place_ref[1], patch)
            new = fresh_refs[patch][1 + part]
            picked = [jnp.where(at == core, new, old) for core, old in enumerate(picked)]
        return jnp.concatenate(picked)

    size = 2 * TOKENS
    blocks = [(at, size, None) for at in range(0, 2 * half, size)]
    if begins:
        blocks[:1] = [(0, TOKENS, 0), (TOKENS, TOKENS, 1)]
    usual = rows_of(0), rows_of(1)

    def scores_of(block):
        at, size, patch = block
        k = usual[0] if patch is None else rows_of(0, patch)
        q = q_refs[at // half][at % half : at % half + size, :]
        return lax.dot_general(q, k, (((1,), (1,)), ((), ())), preferred_element_type=F32)

    def finish(at, size, peak, total, acc):
        total = jnp.sum(total, axis=-1, keepdims=True)
        level = peak + jnp.log2(total)
        high = level.astype(BF16).astype(F32)
        middle = (level - high).astype(BF16).astype(F32)
        low = level - high - middle
        lane = lax.broadcasted_iota(jnp.int32, (size, HEAD), 1)
        packed = jnp.where(lane == 0, high, jnp.where(lane == 1, middle, low))
        out = (acc / total).astype(BF16)
        for g in range(at // TOKENS, (at + size) // TOKENS):
            rows = slice(g * TOKENS - at, (g + 1) * TOKENS - at)
            to = jnp.bitwise_xor(place_ref[1], g % 2) * 4 + jnp.bitwise_xor(place_ref[0], g // 2)
            refs[0][to, :TOKENS, :] = out[rows]
            flat = jnp.transpose(packed[rows])[:8]
            rest = jnp.concatenate([flat[:, HEAD:], jnp.zeros((8, 2 * HEAD - TOKENS), F32)], axis=1)
            refs[0][to, TOKENS:, :] = jnp.concatenate([flat[:, :HEAD], rest]).astype(BF16)

    following = scores_of(blocks[0])
    for index, (at, size, patch) in enumerate(blocks):
        s = following
        if index + 1 < len(blocks):
            following = scores_of(blocks[index + 1])
        rows = slice(at, at + size)
        tiles = [s[:, t * HEAD : (t + 1) * HEAD] for t in range(s.shape[1] // HEAD)]
        peak = jnp.max(functools.reduce(jnp.maximum, tiles), axis=-1, keepdims=True) * scale
        if begins:
            peak = jnp.broadcast_to(peak, (size, HEAD))
        else:
            peak_before = before[0][rows, :]
            peak = jnp.maximum(peak_before, peak)
        tiles = [jnp.exp2(tile * scale - peak) for tile in tiles]
        total = functools.reduce(jnp.add, tiles)
        p = jnp.concatenate([tile.astype(BF16) for tile in tiles], axis=1)
        v = usual[1] if patch is None else rows_of(1, patch)
        acc = jnp.dot(p, v, preferred_element_type=F32)
        if not begins:
            shrink = jnp.exp2(peak_before - peak)
            total += before[1][rows, :] * shrink
            acc += before[2][rows, :] * shrink
        if ends:
            finish(at, size, peak, total, acc)
        else:
            for ref, value in zip(refs, (peak, total, acc), strict=True):
                ref[rows, :] = value


def attend(queries, shares, fresh=(), state=(), place=None, ends=False):
    rows = 2 * queries[0].shape[0]
    begins = bool(fresh)
    operands = [*queries, *fresh, *state, *shares]
    specs = [pl.BlockSpec(memory_space=pltpu.VMEM)] * len(operands)
    if begins or ends:
        operands.insert(0, place)
        specs.insert(0, pl.BlockSpec(memory_space=pltpu.SMEM))
    if ends:
        out_shape = jax.ShapeDtypeStruct((rows // TOKENS, ROWS_SENT, HEAD), BF16)
    else:
        out_shape = (jax.ShapeDtypeStruct((rows, HEAD), F32),) * 3
    key_count = 2 * TOKENS * (1 if ends else len(shares))
    return pl.pallas_call(
        functools.partial(attend_body, len(shares), begins, ends),
        in_specs=specs,
        out_shape=out_shape,
        compiler_params=pltpu.CompilerParams(vmem_limit_bytes=VMEM_LIMIT),
        cost_estimate=pl.CostEstimate(
            flops=4 * rows * key_count * HEAD,
            bytes_accessed=12 * rows * HEAD,
            transcendentals=rows * key_count,
        ),
        name="attend",
    )(*operands)


def merge_body(parts_ref, out_ref):
    count = parts_ref.shape[0]
    chips = count // HEADS_HERE
    weights = []
    for h in range(HEADS_HERE):
        levels = []
        for g in range(h * chips, (h + 1) * chips):
            flat = parts_ref[g, TOKENS:, :].astype(F32)
            wide = jnp.concatenate([flat[:8], flat[8:]], axis=1)
            levels.append(wide[0:1] + wide[1:2] + wide[2:3])
        top = functools.reduce(jnp.maximum, levels)
        weights += [jnp.exp2(one - top) for one in levels]
        whole = sum(weights[h * chips :])
        weights[h * chips :] = [one / whole for one in weights[h * chips :]]
    wide = jnp.concatenate(weights + [jnp.zeros((HEAD - count, 2 * HEAD), F32)])
    columns = jnp.transpose(wide)[:TOKENS]
    for h in range(HEADS_HERE):
        cols = slice(h * HEAD, (h + 1) * HEAD)
        merged = sum(
            columns[:, g : g + 1] * parts_ref[g, :TOKENS, :].astype(F32)
            for g in range(h * chips, (h + 1) * chips)
        ).astype(BF16)
        for copy in range(out_ref.shape[0]):
            out_ref[copy, :, cols] = merged


def merge(parts, copies):
    return pl.pallas_call(
        merge_body,
        out_shape=jax.ShapeDtypeStruct((copies, TOKENS, WIDTH), BF16),
        name="merge",
    )(parts)


def project_body(parts_ref, weight_ref, gate_ref, out_ref):
    acc = jnp.dot(parts_ref[0], weight_ref[:WIDTH], preferred_element_type=F32)
    for g in range(1, parts_ref.shape[0]):
        acc += jnp.dot(
            parts_ref[g], weight_ref[g * WIDTH : (g + 1) * WIDTH], preferred_element_type=F32
        )
    out_ref[...] = (acc * gate_ref[...]).astype(BF16)


def project(parts, out_weight, attn_gate):
    return pl.pallas_call(
        project_body,
        out_shape=jax.ShapeDtypeStruct((TOKENS, out_weight.shape[1]), BF16),
        compiler_params=pltpu.CompilerParams(vmem_limit_bytes=VMEM_LIMIT),
        name="project",
    )(parts, out_weight, attn_gate[None])


def shards(
    query_raw,
    key_raw,
    value_raw,
    stale_pairs,
    query_gain,
    key_gain,
    patch_offsets,
    attn_gate,
    out_weight,
):
    me = lax.axis_index("patch").astype(jnp.int32)
    core = me % 2

    def own_head(both):
        both = jnp.swapaxes(both, 0, 1)
        return lax.dynamic_slice_in_dim(both, core * HEAD, HEAD, axis=3)

    def over_cores(x):
        return lax.all_gather(x, "patch", axis=0, axis_index_groups=CORES)

    share = own_head(over_cores(stale_pairs))
    one, other = ring_swaps(True), ring_swaps(False)
    first = lax.ppermute(share, "patch", other)
    positions = patch_offsets[0] + jnp.arange(TOKENS, dtype=jnp.int32)
    frequency = jnp.exp(
        -(2.0 * jnp.arange(HEAD // 2, dtype=F32) / HEAD) * jnp.log(256.0)
    )
    angles = positions.astype(F32)[:, None] * frequency
    cosine, sine = jnp.cos(angles), jnp.sin(angles)
    fresh_keys, mine, send = prepare(
        core[None],
        query_raw,
        key_raw,
        value_raw,
        query_gain,
        key_gain,
        jnp.concatenate([cosine, cosine], axis=1),
        jnp.concatenate([-sine, sine], axis=1),
    )
    theirs = lax.ppermute(send, "patch", swapped(1))
    share_later, theirs = lax.optimization_barrier((share, theirs))
    second = lax.ppermute(share_later, "patch", one)
    near = jnp.concatenate([mine[0], theirs[0]])
    near = jnp.concatenate([near, lax.ppermute(near, "patch", swapped(2))])
    third = lax.ppermute(first, "patch", one)
    fourth = lax.ppermute(second, "patch", other)
    queries = (near, lax.ppermute(near, "patch", swapped(32)))
    fifth = lax.ppermute(third, "patch", other)
    place = jnp.stack([(me // 32) * 2 + (me // 2) % 2, core])
    state = attend(queries, [share], fresh=(mine, theirs), place=place)
    state = attend(queries, [first, second], state=state)
    fourth, state = lax.optimization_barrier((fourth, state))
    sixth = lax.ppermute(fourth, "patch", one)
    state = attend(queries, [third, fourth], state=state)
    fifth, state = lax.optimization_barrier((fifth, state))
    far_keys = lax.ppermute(fifth[0], "patch", one)
    far_values = lax.ppermute(sixth[1], "patch", other)
    state = attend(queries, [fifth, sixth], state=state)
    parts = attend(queries, [far_keys, far_values], state=state, place=place, ends=True)
    parts = lax.all_to_all(
        parts, "patch", split_axis=0, concat_axis=0, tiled=True, axis_index_groups=QUERY_GROUPS
    )
    copies = merge(parts, 8)
    all_heads = lax.all_to_all(copies, "head", split_axis=0, concat_axis=0, tiled=True)
    return (project(all_heads, out_weight, attn_gate), fresh_keys)


def solution(mesh):
    return jax.shard_map(
        shards,
        mesh=mesh,
        in_specs=(
            P("patch", "head"),
            P("patch", "head"),
            P("patch", "head"),
            P(None, "patch", "head"),
            P(),
            P(),
            P("patch"),
            P("head"),
            P(None, "head"),
        ),
        out_specs=(P("patch", "head"), P("patch", "head")),
        check_vma=False,
    )
```

```python
import functools

import jax
import jax.numpy as jnp
from jax import lax
from jax.experimental import pallas as pl
from jax.experimental.pallas import tpu as pltpu
from jax.sharding import PartitionSpec as P

BF16 = jnp.bfloat16
F32 = jnp.float32
TOKENS = 192
HEAD = 128
WIDTH = 256
HEADS_HERE = 2
STAT_ROWS = 16
ROWS_SENT = TOKENS + STAT_ROWS
LOG2E = 1.4426950408889634
VMEM_LIMIT = 20 * 1024 * 1024

PATCHES = 64
QUERY_GROUPS = [
    [x * 32 + (2 * pair + z) * 2 + core for core in range(2) for x in range(2) for z in range(2)]
    for pair in range(8)
]


def swapped(bit):
    return [(i, i ^ bit) for i in range(PATCHES)]


def ring_swaps(first):
    pairs = []
    for i in range(PATCHES):
        z, core = i % 32 // 2, i % 2
        odd = z // 2 % 2
        by = 2 - 4 * odd if first == (core == 0) else 4 * odd - 2
        pairs.append((i, i // 32 * 32 + (z + by) % 16 * 2 + core))
    return pairs


def prepare_body(
    core_ref, q_ref, k_ref, v_ref, stale_ref, q_gain_ref, k_gain_ref, cos_ref, sin_ref, k_out, mine_out, send_out
):
    cosine = jnp.concatenate([cos_ref[...], cos_ref[...]], axis=1)
    signed_sine = jnp.concatenate([-sin_ref[...], sin_ref[...]], axis=1)
    first = core_ref[0] == 0

    def put(part, heads):
        mine_out[part] = jnp.where(first, heads[0], heads[1])
        send_out[part] = jnp.where(first, heads[1], heads[0])

    for part, (raw, gain) in enumerate(((q_ref, q_gain_ref), (k_ref, k_gain_ref))):
        heads = []
        for h in range(HEADS_HERE):
            cols = slice(h * HEAD, (h + 1) * HEAD)
            x = raw[:, cols].astype(F32)
            squares = jnp.mean(x * x, axis=-1, keepdims=True)
            n = x * lax.rsqrt(squares + 1e-06) * gain[...]
            turned = (n * cosine + pltpu.roll(n, HEAD // 2, 1) * signed_sine).astype(BF16)
            heads.append(turned)
            if part == 1:
                k_out[:, cols] = turned
        put(part, heads)
    put(2, [v_ref[:, :HEAD], v_ref[:, HEAD:]])
    for part in range(2):
        put(3 + part, [stale_ref[part, :, :HEAD], stale_ref[part, :, HEAD:]])


def prepare(core, query_raw, key_raw, value_raw, stale_pairs, query_gain, key_gain, cosine, sine):
    halves = jax.ShapeDtypeStruct((5, TOKENS, HEAD), BF16)
    return pl.pallas_call(
        prepare_body,
        in_specs=[pl.BlockSpec(memory_space=pltpu.SMEM)]
        + [pl.BlockSpec(memory_space=pltpu.VMEM)] * 8,
        out_shape=(jax.ShapeDtypeStruct((TOKENS, WIDTH), BF16), halves, halves),
        name="norm_rotate",
    )(
        core,
        query_raw,
        key_raw,
        value_raw,
        stale_pairs,
        query_gain[None],
        key_gain[None],
        cosine,
        sine,
    )


def attend_body(share_count, begins, ends, *refs):
    refs = list(refs)
    take = lambda count: [refs.pop(0) for _ in range(count)]
    scale = HEAD**-0.5 * LOG2E
    place_ref = take(1)[0] if begins or ends else None
    q_refs = take(2)
    fresh_refs = take(2) if begins else None
    before = None if begins else take(3)
    shares = take(share_count)
    half = q_refs[0].shape[0]

    def rows_of(part, patch=None):
        picked = [share[part, core] for share in shares for core in range(2)]
        if patch is not None:
            picked[patch] = fresh_refs[patch][1 + part]
        return jnp.concatenate(picked)

    size = 2 * TOKENS
    blocks = [(at, size, None) for at in range(0, 2 * half, size)]
    if begins:
        blocks[:1] = [(0, TOKENS, 0), (TOKENS, TOKENS, 1)]
    usual = rows_of(0), rows_of(1)

    def scores_of(block):
        at, size, patch = block
        k = usual[0] if patch is None else rows_of(0, patch)
        q = q_refs[at // half][at % half : at % half + size, :]
        return lax.dot_general(q, k, (((1,), (1,)), ((), ())), preferred_element_type=F32)

    def finish(at, size, peak, total, acc):
        total = jnp.sum(total, axis=-1, keepdims=True)
        level = peak + jnp.log2(total)
        high = level.astype(BF16).astype(F32)
        middle = (level - high).astype(BF16).astype(F32)
        low = level - high - middle
        lane = lax.broadcasted_iota(jnp.int32, (size, HEAD), 1)
        packed = jnp.where(lane == 0, high, jnp.where(lane == 1, middle, low))
        out = (acc / total).astype(BF16)
        for g in range(at // TOKENS, (at + size) // TOKENS):
            rows = slice(g * TOKENS - at, (g + 1) * TOKENS - at)
            to = jnp.bitwise_xor(place_ref[1], g % 2) * 4 + jnp.bitwise_xor(place_ref[0], g // 2)
            refs[0][to, :TOKENS, :] = out[rows]
            flat = jnp.transpose(packed[rows])[:8]
            rest = jnp.concatenate([flat[:, HEAD:], jnp.zeros((8, 2 * HEAD - TOKENS), F32)], axis=1)
            refs[0][to, TOKENS:, :] = jnp.concatenate([flat[:, :HEAD], rest]).astype(BF16)

    following = scores_of(blocks[0])
    for index, (at, size, patch) in enumerate(blocks):
        s = following
        if index + 1 < len(blocks):
            following = scores_of(blocks[index + 1])
        rows = slice(at, at + size)
        tiles = [s[:, t * HEAD : (t + 1) * HEAD] for t in range(s.shape[1] // HEAD)]
        peak = jnp.max(functools.reduce(jnp.maximum, tiles), axis=-1, keepdims=True) * scale
        if begins:
            peak = jnp.broadcast_to(peak, (size, HEAD))
        else:
            peak_before = before[0][rows, :]
            peak = jnp.maximum(peak_before, peak)
        tiles = [jnp.exp2(tile * scale - peak) for tile in tiles]
        total = functools.reduce(jnp.add, tiles)
        p = jnp.concatenate([tile.astype(BF16) for tile in tiles], axis=1)
        v = usual[1] if patch is None else rows_of(1, patch)
        acc = jnp.dot(p, v, preferred_element_type=F32)
        if not begins:
            shrink = jnp.exp2(peak_before - peak)
            total += before[1][rows, :] * shrink
            acc += before[2][rows, :] * shrink
        if ends:
            finish(at, size, peak, total, acc)
        else:
            for ref, value in zip(refs, (peak, total, acc), strict=True):
                ref[rows, :] = value


def attend(queries, shares, fresh=(), state=(), place=None, ends=False):
    rows = 2 * queries[0].shape[0]
    begins = bool(fresh)
    operands = [*queries, *fresh, *state, *shares]
    specs = [pl.BlockSpec(memory_space=pltpu.VMEM)] * len(operands)
    if begins or ends:
        operands.insert(0, place)
        specs.insert(0, pl.BlockSpec(memory_space=pltpu.SMEM))
    if ends:
        out_shape = jax.ShapeDtypeStruct((rows // TOKENS, ROWS_SENT, HEAD), BF16)
    else:
        out_shape = (jax.ShapeDtypeStruct((rows, HEAD), F32),) * 3
    key_count = 2 * TOKENS * len(shares)
    return pl.pallas_call(
        functools.partial(attend_body, len(shares), begins, ends),
        in_specs=specs,
        out_shape=out_shape,
        compiler_params=pltpu.CompilerParams(vmem_limit_bytes=VMEM_LIMIT),
        cost_estimate=pl.CostEstimate(
            flops=4 * rows * key_count * HEAD,
            bytes_accessed=12 * rows * HEAD,
            transcendentals=rows * key_count,
        ),
        name="attend",
    )(*operands)


def merge_body(parts_ref, out_ref):
    count = parts_ref.shape[0]
    chips = count // HEADS_HERE
    weights = []
    for h in range(HEADS_HERE):
        levels = []
        for g in range(h * chips, (h + 1) * chips):
            flat = parts_ref[g, TOKENS:, :].astype(F32)
            wide = jnp.concatenate([flat[:8], flat[8:]], axis=1)
            levels.append(wide[0:1] + wide[1:2] + wide[2:3])
        top = functools.reduce(jnp.maximum, levels)
        weights += [jnp.exp2(one - top) for one in levels]
        whole = sum(weights[h * chips :])
        weights[h * chips :] = [one / whole for one in weights[h * chips :]]
    wide = jnp.concatenate(weights + [jnp.zeros((HEAD - count, 2 * HEAD), F32)])
    columns = jnp.transpose(wide)[:TOKENS]
    for h in range(HEADS_HERE):
        cols = slice(h * HEAD, (h + 1) * HEAD)
        merged = sum(
            columns[:, g : g + 1] * parts_ref[g, :TOKENS, :].astype(F32)
            for g in range(h * chips, (h + 1) * chips)
        ).astype(BF16)
        for copy in range(out_ref.shape[0]):
            out_ref[copy, :, cols] = merged


def merge(parts, copies):
    return pl.pallas_call(
        merge_body,
        out_shape=jax.ShapeDtypeStruct((copies, TOKENS, WIDTH), BF16),
        name="merge",
    )(parts)


def project_body(parts_ref, weight_ref, gate_ref, out_ref):
    acc = jnp.dot(parts_ref[0], weight_ref[:WIDTH], preferred_element_type=F32)
    for g in range(1, parts_ref.shape[0]):
        acc += jnp.dot(
            parts_ref[g], weight_ref[g * WIDTH : (g + 1) * WIDTH], preferred_element_type=F32
        )
    out_ref[...] = (acc * gate_ref[...]).astype(BF16)


def project(parts, out_weight, attn_gate):
    return pl.pallas_call(
        project_body,
        out_shape=jax.ShapeDtypeStruct((TOKENS, out_weight.shape[1]), BF16),
        compiler_params=pltpu.CompilerParams(vmem_limit_bytes=VMEM_LIMIT),
        name="project",
    )(parts, out_weight, attn_gate[None])


def shards(
    query_raw,
    key_raw,
    value_raw,
    stale_pairs,
    query_gain,
    key_gain,
    patch_offsets,
    attn_gate,
    out_weight,
):
    me = lax.axis_index("patch").astype(jnp.int32)
    core = me % 2

    positions = patch_offsets[0] + jnp.arange(TOKENS, dtype=jnp.int32)
    frequency = jnp.exp(
        -(2.0 * jnp.arange(HEAD // 2, dtype=F32) / HEAD) * jnp.log(256.0)
    )
    angles = positions.astype(F32)[:, None] * frequency
    cosine, sine = jnp.cos(angles), jnp.sin(angles)
    fresh_keys, mine, send = prepare(
        core[None],
        query_raw,
        key_raw,
        value_raw,
        stale_pairs,
        query_gain,
        key_gain,
        cosine,
        sine,
    )
    theirs = lax.ppermute(send, "patch", swapped(1))
    share = jnp.stack([mine[3:], theirs[3:]], axis=1)
    one, other = ring_swaps(True), ring_swaps(False)
    first = lax.ppermute(share, "patch", other)
    second = lax.ppermute(share, "patch", one)
    near = jnp.concatenate([mine[0], theirs[0]])
    near = jnp.concatenate([near, lax.ppermute(near, "patch", swapped(2))])
    third = lax.ppermute(first, "patch", one)
    fourth = lax.ppermute(second, "patch", other)
    queries = (near, lax.ppermute(near, "patch", swapped(32)))
    fifth = lax.ppermute(third, "patch", other)
    place = jnp.stack([(me // 32) * 2 + (me // 2) % 2, core])
    state = attend(queries, [share], fresh=(mine, theirs), place=place)
    state = attend(queries, [first, second], state=state)
    fourth, state = lax.optimization_barrier((fourth, state))
    sixth = lax.ppermute(fourth, "patch", one)
    state = attend(queries, [third, fourth], state=state)
    fifth, state = lax.optimization_barrier((fifth, state))
    far = lax.ppermute(fifth, "patch", one)
    state = attend(queries, [fifth, sixth], state=state)
    parts = attend(queries, [far], state=state, place=place, ends=True)
    parts = lax.all_to_all(
        parts, "patch", split_axis=0, concat_axis=0, tiled=True, axis_index_groups=QUERY_GROUPS
    )
    copies = merge(parts, 8)
    all_heads = lax.all_to_all(copies, "head", split_axis=0, concat_axis=0, tiled=True)
    return (project(all_heads, out_weight, attn_gate), fresh_keys)


def solution(mesh):
    return jax.shard_map(
        shards,
        mesh=mesh,
        in_specs=(
            P("patch", "head"),
            P("patch", "head"),
            P("patch", "head"),
            P(None, "patch", "head"),
            P(),
            P(),
            P("patch"),
            P("head"),
            P(None, "head"),
        ),
        out_specs=(P("patch", "head"), P("patch", "head")),
        check_vma=False,
    )
```

```python
import functools

import jax
import jax.numpy as jnp
from jax import lax
from jax.experimental import pallas as pl
from jax.experimental.pallas import tpu as pltpu
from jax.sharding import PartitionSpec as P

BF16 = jnp.bfloat16
F32 = jnp.float32
TOKENS = 192
HEAD = 128
WIDTH = 256
HEADS_HERE = 2
STAT_ROWS = 16
ROWS_SENT = TOKENS + STAT_ROWS
LOG2E = 1.4426950408889634
VMEM_LIMIT = 20 * 1024 * 1024
SMALL = pltpu.CompilerParams(vmem_limit_bytes=8 * 1024 * 1024)

PATCHES = 64
CORES = [[i, i + 1] for i in range(0, PATCHES, 2)]
QUERY_GROUPS = [
    [x * 32 + (2 * pair + z) * 2 + core for core in range(2) for x in range(2) for z in range(2)]
    for pair in range(8)
]


def swapped(bit):
    return [(i, i ^ bit) for i in range(PATCHES)]


def ring_swaps(first):
    pairs = []
    for i in range(PATCHES):
        z, core = i % 32 // 2, i % 2
        odd = z // 2 % 2
        by = 2 - 4 * odd if first == (core == 0) else 4 * odd - 2
        pairs.append((i, i // 32 * 32 + (z + by) % 16 * 2 + core))
    return pairs


def prepare_body(
    q_ref, k_ref, v_ref, stale_ref, q_gain_ref, k_gain_ref, cos_ref, sin_ref, k_out, all_out
):
    cosine = jnp.concatenate([cos_ref[...], cos_ref[...]], axis=1)
    signed_sine = jnp.concatenate([-sin_ref[...], sin_ref[...]], axis=1)
    for part, (raw, gain) in enumerate(((q_ref, q_gain_ref), (k_ref, k_gain_ref))):
        for h in range(HEADS_HERE):
            cols = slice(h * HEAD, (h + 1) * HEAD)
            x = raw[:, cols].astype(F32)
            squares = jnp.mean(x * x, axis=-1, keepdims=True)
            n = x * lax.rsqrt(squares + 1e-06) * gain[...]
            turned = (n * cosine + pltpu.roll(n, HEAD // 2, 1) * signed_sine).astype(BF16)
            all_out[part, :, cols] = turned
            if part == 1:
                k_out[:, cols] = turned
    all_out[2] = v_ref[...]
    all_out[3:] = stale_ref[...]


def prepare(query_raw, key_raw, value_raw, stale_pairs, query_gain, key_gain, cosine, sine):
    return pl.pallas_call(
        prepare_body,
        out_shape=(
            jax.ShapeDtypeStruct((TOKENS, WIDTH), BF16),
            jax.ShapeDtypeStruct((5, TOKENS, WIDTH), BF16),
        ),
        name="norm_rotate",
    )(
        query_raw,
        key_raw,
        value_raw,
        stale_pairs,
        query_gain[None],
        key_gain[None],
        cosine,
        sine,
    )


def attend_body(share_count, begins, ends, *refs):
    refs = list(refs)
    take = lambda count: [refs.pop(0) for _ in range(count)]
    scale = HEAD**-0.5 * LOG2E
    place_ref = take(1)[0] if ends else None
    q_refs = take(2)
    fresh_ref = take(1)[0] if begins else None
    before = None if begins else take(3)
    shares = take(share_count)
    half = q_refs[0].shape[0]

    def rows_of(part, patch=None):
        picked = [share[part, core] for share in shares for core in range(2)]
        if patch is not None:
            picked[patch] = fresh_ref[part, patch]
        return jnp.concatenate(picked)

    size = 2 * TOKENS
    blocks = [(at, size, None) for at in range(0, 2 * half, size)]
    if begins:
        blocks[:1] = [(0, TOKENS, 0), (TOKENS, TOKENS, 1)]
    usual = rows_of(0), rows_of(1)

    def scores_of(block):
        at, size, patch = block
        k = usual[0] if patch is None else rows_of(0, patch)
        q = q_refs[at // half][at % half : at % half + size, :]
        return lax.dot_general(q, k, (((1,), (1,)), ((), ())), preferred_element_type=F32)

    def finish(at, size, peak, total, acc):
        total = jnp.sum(total, axis=-1, keepdims=True)
        level = peak + jnp.log2(total)
        high = level.astype(BF16).astype(F32)
        middle = (level - high).astype(BF16).astype(F32)
        low = level - high - middle
        lane = lax.broadcasted_iota(jnp.int32, (size, HEAD), 1)
        packed = jnp.where(lane == 0, high, jnp.where(lane == 1, middle, low))
        out = (acc / total).astype(BF16)
        for g in range(at // TOKENS, (at + size) // TOKENS):
            rows = slice(g * TOKENS - at, (g + 1) * TOKENS - at)
            to = (g % 2) * 4 + jnp.bitwise_xor(place_ref[0], g // 2)
            refs[0][to, :TOKENS, :] = out[rows]
            flat = jnp.transpose(packed[rows])[:8]
            rest = jnp.concatenate([flat[:, HEAD:], jnp.zeros((8, 2 * HEAD - TOKENS), F32)], axis=1)
            refs[0][to, TOKENS:, :] = jnp.concatenate([flat[:, :HEAD], rest]).astype(BF16)

    following = scores_of(blocks[0])
    for index, (at, size, patch) in enumerate(blocks):
        s = following
        if index + 1 < len(blocks):
            following = scores_of(blocks[index + 1])
        rows = slice(at, at + size)
        tiles = [s[:, t * HEAD : (t + 1) * HEAD] for t in range(s.shape[1] // HEAD)]
        peak = jnp.max(functools.reduce(jnp.maximum, tiles), axis=-1, keepdims=True) * scale
        if begins:
            peak = jnp.broadcast_to(peak, (size, HEAD))
        else:
            peak_before = before[0][rows, :]
            peak = jnp.maximum(peak_before, peak)
        tiles = [jnp.exp2(tile * scale - peak) for tile in tiles]
        total = functools.reduce(jnp.add, tiles)
        p = jnp.concatenate([tile.astype(BF16) for tile in tiles], axis=1)
        v = usual[1] if patch is None else rows_of(1, patch)
        acc = jnp.dot(p, v, preferred_element_type=F32)
        if not begins:
            shrink = jnp.exp2(peak_before - peak)
            total += before[1][rows, :] * shrink
            acc += before[2][rows, :] * shrink
        if ends:
            finish(at, size, peak, total, acc)
        else:
            for ref, value in zip(refs, (peak, total, acc), strict=True):
                ref[rows, :] = value


def attend(queries, shares, fresh=None, state=(), place=None):
    rows = 2 * queries[0].shape[0]
    begins, ends = fresh is not None, place is not None
    operands = [*queries, *([fresh] if begins else []), *state, *shares]
    specs = [pl.BlockSpec(memory_space=pltpu.VMEM)] * len(operands)
    if ends:
        operands.insert(0, place)
        specs.insert(0, pl.BlockSpec(memory_space=pltpu.SMEM))
        out_shape = jax.ShapeDtypeStruct((rows // TOKENS, ROWS_SENT, HEAD), BF16)
    else:
        out_shape = (jax.ShapeDtypeStruct((rows, HEAD), F32),) * 3
    key_count = 2 * TOKENS * len(shares)
    return pl.pallas_call(
        functools.partial(attend_body, len(shares), begins, ends),
        in_specs=specs,
        out_shape=out_shape,
        compiler_params=pltpu.CompilerParams(vmem_limit_bytes=VMEM_LIMIT),
        cost_estimate=pl.CostEstimate(
            flops=4 * rows * key_count * HEAD,
            bytes_accessed=12 * rows * HEAD,
            transcendentals=rows * key_count,
        ),
        name="attend",
    )(*operands)


def merge_body(parts_ref, out_ref):
    count = parts_ref.shape[0]
    chips = count // HEADS_HERE
    weights = []
    for h in range(HEADS_HERE):
        levels = []
        for g in range(h * chips, (h + 1) * chips):
            flat = parts_ref[g, TOKENS:, :].astype(F32)
            wide = jnp.concatenate([flat[:8], flat[8:]], axis=1)
            levels.append(wide[0:1] + wide[1:2] + wide[2:3])
        top = functools.reduce(jnp.maximum, levels)
        weights += [jnp.exp2(one - top) for one in levels]
        whole = sum(weights[h * chips :])
        weights[h * chips :] = [one / whole for one in weights[h * chips :]]
    wide = jnp.concatenate(weights + [jnp.zeros((HEAD - count, 2 * HEAD), F32)])
    columns = jnp.transpose(wide)[:TOKENS]
    for h in range(HEADS_HERE):
        cols = slice(h * HEAD, (h + 1) * HEAD)
        merged = sum(
            columns[:, g : g + 1] * parts_ref[g, :TOKENS, :].astype(F32)
            for g in range(h * chips, (h + 1) * chips)
        ).astype(BF16)
        for copy in range(out_ref.shape[0]):
            out_ref[copy, :, cols] = merged


def merge(parts, copies):
    return pl.pallas_call(
        merge_body,
        out_shape=jax.ShapeDtypeStruct((copies, TOKENS, WIDTH), BF16),
        compiler_params=SMALL,
        name="merge",
    )(parts)


def project_body(parts_ref, weight_ref, gate_ref, out_ref):
    acc = jnp.dot(parts_ref[0], weight_ref[:WIDTH], preferred_element_type=F32)
    for g in range(1, parts_ref.shape[0]):
        acc += jnp.dot(
            parts_ref[g], weight_ref[g * WIDTH : (g + 1) * WIDTH], preferred_element_type=F32
        )
    out_ref[...] = (acc * gate_ref[...]).astype(BF16)


def project(parts, out_weight, attn_gate):
    return pl.pallas_call(
        project_body,
        out_shape=jax.ShapeDtypeStruct((TOKENS, out_weight.shape[1]), BF16),
        compiler_params=SMALL,
        name="project",
    )(parts, out_weight, attn_gate[None])


def shards(
    query_raw,
    key_raw,
    value_raw,
    stale_pairs,
    query_gain,
    key_gain,
    patch_offsets,
    attn_gate,
    out_weight,
):
    me = lax.axis_index("patch").astype(jnp.int32)
    core = me % 2

    positions = patch_offsets[0] + jnp.arange(TOKENS, dtype=jnp.int32)
    frequency = jnp.exp(
        -(2.0 * jnp.arange(HEAD // 2, dtype=F32) / HEAD) * jnp.log(256.0)
    )
    angles = positions.astype(F32)[:, None] * frequency
    cosine, sine = jnp.cos(angles), jnp.sin(angles)
    fresh_keys, prepared = prepare(
        query_raw, key_raw, value_raw, stale_pairs, query_gain, key_gain, cosine, sine
    )
    rows = lax.all_gather(prepared, "patch", axis=0, axis_index_groups=CORES)
    rows = jnp.swapaxes(rows, 0, 1)
    rows = lax.dynamic_slice_in_dim(rows, core * HEAD, HEAD, axis=3)
    near, fresh, share = rows[0].reshape(2 * TOKENS, HEAD), rows[1:3], rows[3:]
    one, other = ring_swaps(True), ring_swaps(False)
    first = lax.ppermute(share, "patch", other)
    second = lax.ppermute(share, "patch", one)
    near = jnp.concatenate([near, lax.ppermute(near, "patch", swapped(2))])
    third = lax.ppermute(first, "patch", one)
    fourth = lax.ppermute(second, "patch", other)
    queries = (near, lax.ppermute(near, "patch", swapped(32)))
    fifth = lax.ppermute(third, "patch", other)
    place = ((me // 32) * 2 + (me // 2) % 2)[None]
    state = attend(queries, [share], fresh=fresh)
    state = attend(queries, [first, second], state=state)
    fourth, state = lax.optimization_barrier((fourth, state))
    sixth = lax.ppermute(fourth, "patch", one)
    state = attend(queries, [third, fourth], state=state)
    fifth, state = lax.optimization_barrier((fifth, state))
    far = lax.ppermute(fifth, "patch", one)
    state = attend(queries, [fifth, sixth], state=state)
    parts = attend(queries, [far], state=state, place=place)
    parts = lax.all_to_all(
        parts, "patch", split_axis=0, concat_axis=0, tiled=True, axis_index_groups=QUERY_GROUPS
    )
    copies = merge(parts, 8)
    all_heads = lax.all_to_all(copies, "head", split_axis=0, concat_axis=0, tiled=True)
    return (project(all_heads, out_weight, attn_gate), fresh_keys)


def solution(mesh):
    return jax.shard_map(
        shards,
        mesh=mesh,
        in_specs=(
            P("patch", "head"),
            P("patch", "head"),
            P("patch", "head"),
            P(None, "patch", "head"),
            P(),
            P(),
            P("patch"),
            P("head"),
            P(None, "head"),
        ),
        out_specs=(P("patch", "head"), P("patch", "head")),
        check_vma=False,
    )
```

```python
import functools

import jax
import jax.numpy as jnp
import numpy as np
from jax import lax
from jax.experimental import pallas as pl
from jax.experimental.pallas import tpu as pltpu
from jax.sharding import PartitionSpec as P

BF16 = jnp.bfloat16
F32 = jnp.float32
TOKENS = 192
HEAD = 128
WIDTH = 256
HEADS_HERE = 2
STAT_ROWS = 16
ROWS_SENT = TOKENS + STAT_ROWS
LOG2E = 1.4426950408889634
VMEM_LIMIT = 20 * 1024 * 1024
SMALL = pltpu.CompilerParams(vmem_limit_bytes=8 * 1024 * 1024)

PATCHES = 64
CORES = [[i, i + 1] for i in range(0, PATCHES, 2)]
QUERY_GROUPS = [
    [x * 32 + (2 * pair + z) * 2 + core for core in range(2) for x in range(2) for z in range(2)]
    for pair in range(8)
]


def swapped(bit):
    return [(i, i ^ bit) for i in range(PATCHES)]


def ring_swaps(first):
    pairs = []
    for i in range(PATCHES):
        z, core = i % 32 // 2, i % 2
        odd = z // 2 % 2
        by = 2 - 4 * odd if first == (core == 0) else 4 * odd - 2
        pairs.append((i, i // 32 * 32 + (z + by) % 16 * 2 + core))
    return pairs


def prepare_body(
    offset_ref, q_ref, k_ref, v_ref, stale_ref, q_gain_ref, k_gain_ref, k_out, all_out
):
    half = HEAD // 2
    lane = lax.broadcasted_iota(jnp.int32, (TOKENS, HEAD), 1)
    place = jnp.where(lane < half, lane, lane - half).astype(F32)
    frequency = jnp.exp(-(2.0 * place / HEAD) * np.float32(np.log(256.0)))
    positions = offset_ref[0] + lax.broadcasted_iota(jnp.int32, (TOKENS, HEAD), 0)
    angles = positions.astype(F32) * frequency
    cosine, sine = jnp.cos(angles), jnp.sin(angles)
    signed_sine = jnp.where(lane < half, -sine, sine)
    for part, (raw, gain) in enumerate(((q_ref, q_gain_ref), (k_ref, k_gain_ref))):
        for h in range(HEADS_HERE):
            cols = slice(h * HEAD, (h + 1) * HEAD)
            x = raw[:, cols].astype(F32)
            squares = jnp.mean(x * x, axis=-1, keepdims=True)
            n = x * lax.rsqrt(squares + 1e-06) * gain[...]
            turned = (n * cosine + pltpu.roll(n, HEAD // 2, 1) * signed_sine).astype(BF16)
            all_out[part, :, cols] = turned
            if part == 1:
                k_out[:, cols] = turned
    all_out[2] = v_ref[...]
    all_out[3:] = stale_ref[...]


def prepare(patch_offsets, query_raw, key_raw, value_raw, stale_pairs, query_gain, key_gain):
    return pl.pallas_call(
        prepare_body,
        in_specs=[pl.BlockSpec(memory_space=pltpu.SMEM)]
        + [pl.BlockSpec(memory_space=pltpu.VMEM)] * 6,
        out_shape=(
            jax.ShapeDtypeStruct((TOKENS, WIDTH), BF16),
            jax.ShapeDtypeStruct((5, TOKENS, WIDTH), BF16),
        ),
        name="norm_rotate",
    )(
        patch_offsets,
        query_raw,
        key_raw,
        value_raw,
        stale_pairs,
        query_gain[None],
        key_gain[None],
    )


def attend_body(share_count, begins, ends, *refs):
    refs = list(refs)
    take = lambda count: [refs.pop(0) for _ in range(count)]
    scale = HEAD**-0.5 * LOG2E
    place_ref = take(1)[0] if ends else None
    q_refs = take(2)
    fresh_ref = take(1)[0] if begins else None
    before = None if begins else take(3)
    shares = take(share_count)
    half = q_refs[0].shape[0]

    def rows_of(part, patch=None):
        picked = [share[part, core] for share in shares for core in range(2)]
        if patch is not None:
            picked[patch] = fresh_ref[part, patch]
        return jnp.concatenate(picked)

    size = 2 * TOKENS
    blocks = [(at, size, None) for at in range(0, 2 * half, size)]
    if begins:
        blocks[:1] = [(0, TOKENS, 0), (TOKENS, TOKENS, 1)]
    usual = rows_of(0), rows_of(1)

    def scores_of(block):
        at, size, patch = block
        k = usual[0] if patch is None else rows_of(0, patch)
        q = q_refs[at // half][at % half : at % half + size, :]
        return lax.dot_general(q, k, (((1,), (1,)), ((), ())), preferred_element_type=F32)

    def finish(at, size, peak, total, acc):
        total = jnp.sum(total, axis=-1, keepdims=True)
        level = peak + jnp.log2(total)
        high = level.astype(BF16).astype(F32)
        middle = (level - high).astype(BF16).astype(F32)
        low = level - high - middle
        lane = lax.broadcasted_iota(jnp.int32, (size, HEAD), 1)
        packed = jnp.where(lane == 0, high, jnp.where(lane == 1, middle, low))
        out = (acc / total).astype(BF16)
        for g in range(at // TOKENS, (at + size) // TOKENS):
            rows = slice(g * TOKENS - at, (g + 1) * TOKENS - at)
            to = (g % 2) * 4 + jnp.bitwise_xor(place_ref[0], g // 2)
            refs[0][to, :TOKENS, :] = out[rows]
            flat = jnp.transpose(packed[rows])[:8]
            rest = jnp.concatenate([flat[:, HEAD:], jnp.zeros((8, 2 * HEAD - TOKENS), F32)], axis=1)
            refs[0][to, TOKENS:, :] = jnp.concatenate([flat[:, :HEAD], rest]).astype(BF16)

    following = scores_of(blocks[0])
    for index, (at, size, patch) in enumerate(blocks):
        s = following
        if index + 1 < len(blocks):
            following = scores_of(blocks[index + 1])
        rows = slice(at, at + size)
        tiles = [s[:, t * HEAD : (t + 1) * HEAD] for t in range(s.shape[1] // HEAD)]
        peak = jnp.max(functools.reduce(jnp.maximum, tiles), axis=-1, keepdims=True) * scale
        if begins:
            peak = jnp.broadcast_to(peak, (size, HEAD))
        else:
            peak_before = before[0][rows, :]
            peak = jnp.maximum(peak_before, peak)
        tiles = [jnp.exp2(tile * scale - peak) for tile in tiles]
        total = functools.reduce(jnp.add, tiles)
        p = jnp.concatenate([tile.astype(BF16) for tile in tiles], axis=1)
        v = usual[1] if patch is None else rows_of(1, patch)
        acc = jnp.dot(p, v, preferred_element_type=F32)
        if not begins:
            shrink = jnp.exp2(peak_before - peak)
            total += before[1][rows, :] * shrink
            acc += before[2][rows, :] * shrink
        if ends:
            finish(at, size, peak, total, acc)
        else:
            for ref, value in zip(refs, (peak, total, acc), strict=True):
                ref[rows, :] = value


def attend(queries, shares, fresh=None, state=(), place=None):
    rows = 2 * queries[0].shape[0]
    begins, ends = fresh is not None, place is not None
    operands = [*queries, *([fresh] if begins else []), *state, *shares]
    specs = [pl.BlockSpec(memory_space=pltpu.VMEM)] * len(operands)
    if ends:
        operands.insert(0, place)
        specs.insert(0, pl.BlockSpec(memory_space=pltpu.SMEM))
        out_shape = jax.ShapeDtypeStruct((rows // TOKENS, ROWS_SENT, HEAD), BF16)
    else:
        out_shape = (jax.ShapeDtypeStruct((rows, HEAD), F32),) * 3
    key_count = 2 * TOKENS * len(shares)
    return pl.pallas_call(
        functools.partial(attend_body, len(shares), begins, ends),
        in_specs=specs,
        out_shape=out_shape,
        compiler_params=pltpu.CompilerParams(vmem_limit_bytes=VMEM_LIMIT),
        cost_estimate=pl.CostEstimate(
            flops=4 * rows * key_count * HEAD,
            bytes_accessed=12 * rows * HEAD,
            transcendentals=rows * key_count,
        ),
        name="attend",
    )(*operands)


def merge_body(parts_ref, out_ref):
    count = parts_ref.shape[0]
    chips = count // HEADS_HERE
    weights = []
    for h in range(HEADS_HERE):
        levels = []
        for g in range(h * chips, (h + 1) * chips):
            flat = parts_ref[g, TOKENS:, :].astype(F32)
            wide = jnp.concatenate([flat[:8], flat[8:]], axis=1)
            levels.append(wide[0:1] + wide[1:2] + wide[2:3])
        top = functools.reduce(jnp.maximum, levels)
        weights += [jnp.exp2(one - top) for one in levels]
        whole = sum(weights[h * chips :])
        weights[h * chips :] = [one / whole for one in weights[h * chips :]]
    wide = jnp.concatenate(weights + [jnp.zeros((HEAD - count, 2 * HEAD), F32)])
    columns = jnp.transpose(wide)[:TOKENS]
    for h in range(HEADS_HERE):
        cols = slice(h * HEAD, (h + 1) * HEAD)
        merged = sum(
            columns[:, g : g + 1] * parts_ref[g, :TOKENS, :].astype(F32)
            for g in range(h * chips, (h + 1) * chips)
        ).astype(BF16)
        for copy in range(out_ref.shape[0]):
            out_ref[copy, :, cols] = merged


def merge(parts, copies):
    return pl.pallas_call(
        merge_body,
        out_shape=jax.ShapeDtypeStruct((copies, TOKENS, WIDTH), BF16),
        compiler_params=SMALL,
        name="merge",
    )(parts)


def project_body(parts_ref, weight_ref, gate_ref, out_ref):
    acc = jnp.dot(parts_ref[0], weight_ref[:WIDTH], preferred_element_type=F32)
    for g in range(1, parts_ref.shape[0]):
        acc += jnp.dot(
            parts_ref[g], weight_ref[g * WIDTH : (g + 1) * WIDTH], preferred_element_type=F32
        )
    out_ref[...] = (acc * gate_ref[...]).astype(BF16)


def project(parts, out_weight, attn_gate):
    return pl.pallas_call(
        project_body,
        out_shape=jax.ShapeDtypeStruct((TOKENS, out_weight.shape[1]), BF16),
        compiler_params=SMALL,
        name="project",
    )(parts, out_weight, attn_gate[None])


def shards(
    query_raw,
    key_raw,
    value_raw,
    stale_pairs,
    query_gain,
    key_gain,
    patch_offsets,
    attn_gate,
    out_weight,
):
    me = lax.axis_index("patch").astype(jnp.int32)
    core = me % 2

    fresh_keys, prepared = prepare(
        patch_offsets, query_raw, key_raw, value_raw, stale_pairs, query_gain, key_gain
    )
    rows = lax.all_gather(prepared, "patch", axis=0, axis_index_groups=CORES)
    rows = jnp.swapaxes(rows, 0, 1)
    rows = lax.dynamic_slice_in_dim(rows, core * HEAD, HEAD, axis=3)
    near, fresh, share = rows[0].reshape(2 * TOKENS, HEAD), rows[1:3], rows[3:]
    one, other = ring_swaps(True), ring_swaps(False)
    first = lax.ppermute(share, "patch", other)
    second = lax.ppermute(share, "patch", one)
    near = jnp.concatenate([near, lax.ppermute(near, "patch", swapped(2))])
    third = lax.ppermute(first, "patch", one)
    fourth = lax.ppermute(second, "patch", other)
    queries = (near, lax.ppermute(near, "patch", swapped(32)))
    fifth = lax.ppermute(third, "patch", other)
    place = ((me // 32) * 2 + (me // 2) % 2)[None]
    state = attend(queries, [share], fresh=fresh)
    state = attend(queries, [first, second], state=state)
    fourth, state = lax.optimization_barrier((fourth, state))
    sixth = lax.ppermute(fourth, "patch", one)
    state = attend(queries, [third, fourth], state=state)
    fifth, state = lax.optimization_barrier((fifth, state))
    far = lax.ppermute(fifth, "patch", one)
    state = attend(queries, [fifth, sixth], state=state)
    parts = attend(queries, [far], state=state, place=place)
    parts = lax.all_to_all(
        parts, "patch", split_axis=0, concat_axis=0, tiled=True, axis_index_groups=QUERY_GROUPS
    )
    copies = merge(parts, 8)
    all_heads = lax.all_to_all(copies, "head", split_axis=0, concat_axis=0, tiled=True)
    return (project(all_heads, out_weight, attn_gate), fresh_keys)


def solution(mesh):
    return jax.shard_map(
        shards,
        mesh=mesh,
        in_specs=(
            P("patch", "head"),
            P("patch", "head"),
            P("patch", "head"),
            P(None, "patch", "head"),
            P(),
            P(),
            P("patch"),
            P("head"),
            P(None, "head"),
        ),
        out_specs=(P("patch", "head"), P("patch", "head")),
        check_vma=False,
    )
```
